32 devices in a mesh: dp: 4 (over y, x), ctx: 4 (over z), tp: 2 (over core).
Axes of the slice: x: 2, y: 2, z: 4, core: 2. Of those that a mesh axis runs over, the one named last changes fastest.
Arguments:
- tokens: bfloat16 [4, 4, 1024, 1024], P(None, 'dp', 'ctx', 'tp'), may hold values from -6 to 6
- segments: int32 [4, 4, 1024], P(None, 'dp'), may hold values from 0 to 1023, as said below
- first_gain: float32 [1024], replicated, may hold values from 0.1 to 1.9
- query_weight: bfloat16 [1024, 512], P(('dp', 'ctx'), 'tp'), may hold values from -0.1875 to 0.1875
- key_weight: bfloat16 [1024, 512], P(('dp', 'ctx'), 'tp'), may hold values from -0.1875 to 0.1875
- value_weight: bfloat16 [1024, 1024], P(('dp', 'ctx'), 'tp'), may hold values from -0.1875 to 0.1875
- gate_weight: bfloat16 [1024, 1024], P(('dp', 'ctx'), 'tp'), may hold values from -0.1875 to 0.1875
- beta_weight: bfloat16 [1024, 4], P(('dp', 'ctx'), 'tp'), may hold values from -0.1875 to 0.1875
- decay_weight: bfloat16 [1024, 4], P(('dp', 'ctx'), 'tp'), may hold values from -0.1875 to 0.1875
- conv_query: float32 [4, 512], replicated, may hold values from -3 to 3
- conv_key: float32 [4, 512], replicated, may hold values from -3 to 3
- conv_value: float32 [4, 1024], replicated, may hold values from -3 to 3
- decay_log: float32 [4], replicated, may hold values from -5 to 0.5
- decay_bias: float32 [4], replicated, may hold values from -3 to 1
- output_gain: float32 [256], replicated, may hold values from 0.1 to 1.9
- out_weight: bfloat16 [1024, 1024], P('tp', ('dp', 'ctx')), may hold values from -0.375 to 0.375
- second_gain: float32 [1024], replicated, may hold values from 0.1 to 1.9
- ffn_gate: bfloat16 [1024, 2816], P(('dp', 'ctx'), 'tp'), may hold values from -0.1875 to 0.1875
- ffn_up: bfloat16 [1024, 2816], P(('dp', 'ctx'), 'tp'), may hold values from -0.1875 to 0.1875
- ffn_down: bfloat16 [2816, 1024], P('tp', ('dp', 'ctx')), may hold values from -0.21875 to 0.21875
- out_grad: bfloat16 [4, 4, 1024, 1024], P(None, 'dp', 'ctx'), may hold values from -6 to 6
Outputs:
- layer_out: bfloat16 [4, 4, 1024, 1024], P(None, 'dp', 'ctx', 'tp')
- token_grad: float32 [4, 4, 1024, 1024], P(None, 'dp', 'ctx', 'tp')
- grad_first_gain: float32 [1024], replicated
- grad_query_weight: float32 [1024, 512], P(('dp', 'ctx'), 'tp')
- grad_key_weight: float32 [1024, 512], P(('dp', 'ctx'), 'tp')
- grad_value_weight: float32 [1024, 1024], P(('dp', 'ctx'), 'tp')
- grad_gate_weight: float32 [1024, 1024], P(('dp', 'ctx'), 'tp')
- grad_beta_weight: float32 [1024, 4], P(('dp', 'ctx'), 'tp')
- grad_decay_weight: float32 [1024, 4], P(('dp', 'ctx'), 'tp')
- grad_conv_query: float32 [4, 512], replicated
- grad_conv_key: float32 [4, 512], replicated
- grad_conv_value: float32 [4, 1024], replicated
- grad_decay_log: float32 [4], replicated
- grad_decay_bias: float32 [4], replicated
- grad_output_gain: float32 [256], replicated
- grad_out_weight: float32 [1024, 1024], P('tp', ('dp', 'ctx'))
- grad_second_gain: float32 [1024], replicated
- grad_ffn_gate: float32 [1024, 2816], P(('dp', 'ctx'), 'tp')
- grad_ffn_up: float32 [1024, 2816], P(('dp', 'ctx'), 'tp')
- grad_ffn_down: float32 [2816, 1024], P('tp', ('dp', 'ctx'))
The draws below stay inside these ranges and needn't reach their ends.
Inputs may be any that keep to these rules, and one draw needn't show every extreme that they name: `segments`: along each sequence the ids never fall; a document's id is the position of its first token in the sequence, and the last token of every sequence is a document of its own.
All inputs are finite; a program needn't handle non-finite values.
Results may differ from the reference program's by a relative error of at most 0.012.
Values may be sent and summed in bfloat16 or wider, within the bound.
A program may use at most 256 MiB of HBM per device.

```python
import jax
import jax.numpy as jnp
from jax import lax

D = 1024
H = 4
DK = 128
DV = 256
FF = 2816
CONV = 4
BLOCK = 64
MICRO = 4
SEQ_DEV = 256
LENGTH = 1024
SEQS = 4


def draw_segments(key, part):
    key = jax.random.fold_in(key, 11)
    start_key, stop_key, coin_key = jax.random.split(key, 3)
    row_count = MICRO * SEQS
    long_start = jax.random.randint(start_key, (row_count, 1), 1, SEQ_DEV)
    long_stop = jax.random.randint(stop_key, (row_count, 1), LENGTH - SEQ_DEV + 1, LENGTH)
    position = jnp.arange(LENGTH, dtype=jnp.int32)[None, :]
    coins = jax.random.randint(coin_key, (row_count, LENGTH), 0, 24) == 0
    outside = (position < long_start) | (position > long_stop)
    flags = coins & outside | (position == long_start) | (position == long_stop) | (position == LENGTH - 1)
    flags = flags & (position > 0)
    starts = jnp.where(flags, position, jnp.zeros_like(position))
    starts = jnp.broadcast_to(starts, (row_count, LENGTH)).astype(jnp.int32)
    ids = lax.cummax(starts, axis=1)
    return ids.reshape(MICRO, SEQS, LENGTH)


def shard_levels(own_key, extent, shards, least, high):
    gain = 1.0
    for dim, blocks in shards:
        steps = jax.random.uniform(jax.random.fold_in(jax.random.fold_in(own_key, 6), dim), (blocks,), jnp.float32, least / len(shards), high / len(shards))
        gain = gain * jnp.repeat(jnp.exp(steps), extent[dim] // blocks).reshape((-1,) + (1,) * (len(extent) - 1 - dim))
    return gain


def gaussian(key, shape, scale, reach, cuts=(), kind=jnp.bfloat16):
    loudness = shard_levels(key, shape, cuts, -0.22, 0.18) if cuts else 1.0
    result = jax.random.normal(key, shape, jnp.float32) * scale * loudness
    return jnp.minimum(jnp.maximum(result, -reach), reach).astype(kind)


def setup_inputs(seed: int = 0) -> dict:
    key_list = jax.random.split(jax.random.key(seed), 22)
    tokens = gaussian(key_list[0], (MICRO, SEQS, LENGTH, D), 1.0, 6.0, ((1, 4), (2, 4), (3, 2)))
    segments = draw_segments(jax.random.fold_in(key_list[21], 71), 0)
    first_gain = jnp.clip(1.0 + 0.18 * jax.random.normal(key_list[2], (D,), jnp.float32), 0.1, 1.9)
    query_weight = gaussian(key_list[3], (D, H * DK), D ** -0.5, 0.1875, ((0, 16), (1, 2)))
    key_weight = gaussian(key_list[4], (D, H * DK), D ** -0.5, 0.1875, ((0, 16), (1, 2)))
    value_weight = gaussian(key_list[5], (D, H * DV), D ** -0.5, 0.1875, ((0, 16), (1, 2)))
    gate_weight = gaussian(key_list[6], (D, H * DV), D ** -0.5, 0.1875, ((0, 16), (1, 2)))
    beta_weight = gaussian(key_list[7], (D, H), D ** -0.5, 0.1875, ((0, 16), (1, 2)))
    decay_weight = gaussian(key_list[8], (D, H), D ** -0.5, 0.1875, ((0, 16), (1, 2)))
    conv_query = gaussian(key_list[9], (CONV, H * DK), 0.5, 3.0, (), jnp.float32)
    conv_key = gaussian(key_list[10], (CONV, H * DK), 0.5, 3.0, (), jnp.float32)
    conv_value = gaussian(key_list[11], (CONV, H * DV), 0.5, 3.0, (), jnp.float32)
    decay_log = jnp.clip(jax.random.uniform(key_list[12], (H,), jnp.float32, -5.0, 0.5), -5.0, 0.5)
    decay_bias = jnp.clip(jax.random.uniform(key_list[13], (H,), jnp.float32, -3.0, 1.0), -3.0, 1.0)
    output_gain = jnp.clip(1.0 + 0.18 * jax.random.normal(key_list[14], (DV,), jnp.float32), 0.1, 1.9)
    out_weight = gaussian(key_list[15], (H * DV, D), (H * DV // 4) ** -0.5, 0.375, ((0, 2), (1, 16)))
    second_gain = jnp.clip(1.0 + 0.18 * jax.random.normal(key_list[16], (D,), jnp.float32), 0.1, 1.9)
    ffn_gate = gaussian(key_list[17], (D, FF), D ** -0.5, 0.1875, ((0, 16), (1, 2)))
    ffn_up = gaussian(key_list[18], (D, FF), D ** -0.5, 0.1875, ((0, 16), (1, 2)))
    ffn_down = gaussian(key_list[19], (FF, D), (FF // 4) ** -0.5, 0.21875, ((0, 2), (1, 16)))
    out_grad = gaussian(key_list[20], (MICRO, SEQS, LENGTH, D), 1.0, 6.0, ((1, 4), (2, 4)))
    return {"tokens": tokens, "segments": segments, "first_gain": first_gain, "query_weight": query_weight, "key_weight": key_weight, "value_weight": value_weight, "gate_weight": gate_weight, "beta_weight": beta_weight, "decay_weight": decay_weight, "conv_query": conv_query, "conv_key": conv_key, "conv_value": conv_value, "decay_log": decay_log, "decay_bias": decay_bias, "output_gain": output_gain, "out_weight": out_weight, "second_gain": second_gain, "ffn_gate": ffn_gate, "ffn_up": ffn_up, "ffn_down": ffn_down, "out_grad": out_grad}


exact_precision = lax.Precision.HIGHEST

@jax.custom_vjp
def low(v):
    return lax.optimization_barrier(v.astype(jnp.bfloat16)).astype(jnp.float32)

@jax.custom_vjp
def low_back(v):
    return v

def low_keep(v):
    return (low(v), None)

def low_pass(kept, grad):
    return (grad,)

def back_keep(v):
    return (v, None)

def back_low(kept, grad):
    return (low(grad),)
low.defvjp(low_keep, low_pass)
low_back.defvjp(back_keep, back_low)

def mult(left_side, right_side):
    return jnp.dot(left_side.astype(jnp.float32), right_side.astype(jnp.float32), preferred_element_type=jnp.float32, precision=exact_precision)

def rms_scale(values, gain_row):
    return values * lax.rsqrt(lax.optimization_barrier(jnp.mean(values * values, axis=-1, keepdims=True)) + 1e-06) * gain_row

def unit_norm(values):
    return values * lax.rsqrt(lax.optimization_barrier(jnp.sum(values * values, axis=-1, keepdims=True)) + 1e-06)

def lower_solve(system, right_rows):
    return lax.linalg.triangular_solve(system, right_rows, left_side=True, lower=True, unit_diagonal=True)

def conv_mix(padded, weight_taps, seg_pad):
    row_count = padded.shape[0] - CONV + 1
    seg_here = seg_pad[CONV - 1:]
    summed = jnp.zeros((row_count, padded.shape[1]), jnp.float32)
    for offset in range(CONV):
        first_row = CONV - 1 - offset
        same_doc = (seg_pad[first_row:first_row + row_count] == seg_here).astype(jnp.float32)
        summed = summed + weight_taps[offset] * padded[first_row:first_row + row_count] * same_doc[:, None]
    return summed

def split_heads(values, head_count):
    row_count, col_count = values.shape
    shaped = values.reshape(row_count // BLOCK, BLOCK, head_count, col_count // head_count)
    return jnp.transpose(shaped, (2, 0, 1, 3))

def block_prep(query_rows, key_rows, value_rows, beta_rows, rate_rows, seg_blocks, seg_before):
    block_size = rate_rows.shape[-1]
    cumulative = jnp.cumsum(rate_rows, axis=-1)
    lower_mask = jnp.tril(jnp.ones((block_size, block_size), dtype=bool))
    visible = lower_mask[None, None] & (seg_blocks[:, :, None] == seg_blocks[:, None, :])[None]
    log_ratio = cumulative[..., :, None] - cumulative[..., None, :]
    decay = jnp.where(visible, jnp.exp(jnp.where(visible, log_ratio, 0.0)), 0.0)
    start_same = (seg_blocks == seg_before[:, None]).astype(jnp.float32)
    gamma_in = jnp.exp(cumulative) * start_same[None]
    end_same = (seg_blocks == seg_blocks[:, -1:]).astype(jnp.float32)
    to_end = jnp.exp(cumulative[..., -1:] - cumulative) * end_same[None]
    gamma_all = jnp.exp(cumulative[..., -1]) * (seg_blocks[:, -1] == seg_before).astype(jnp.float32)[None]
    key_inner = jnp.einsum('hnid,hnjd->hnij', key_rows, key_rows, precision=exact_precision)
    identity = jnp.eye(block_size, dtype=jnp.float32)
    strict = decay * (1.0 - identity)
    system = identity + beta_rows[..., :, None] * strict * key_inner
    solved_keys = lower_solve(system, (beta_rows * gamma_in)[..., None] * key_rows)
    solved_values = lower_solve(system, beta_rows[..., None] * value_rows)
    scores = jnp.einsum('hnid,hnjd->hnij', query_rows, key_rows, precision=exact_precision) * decay
    return (solved_keys, solved_values, scores, gamma_in, to_end, gamma_all, query_rows, key_rows)

def mixer_inputs(in_query, in_key, in_value, in_beta, in_decay, pad_query, pad_key, pad_value, tap_query, tap_key, tap_value, log_rate, bias_rate, seg_pad, seg_blocks, seg_before):
    head_count = log_rate.shape[0]
    block_count = seg_blocks.shape[0]
    query_rows = jax.nn.silu(conv_mix(jnp.concatenate([pad_query, in_query], axis=0), tap_query, seg_pad))
    key_rows = jax.nn.silu(conv_mix(jnp.concatenate([pad_key, in_key], axis=0), tap_key, seg_pad))
    value_rows = jax.nn.silu(conv_mix(jnp.concatenate([pad_value, in_value], axis=0), tap_value, seg_pad))
    query_rows = unit_norm(split_heads(query_rows, head_count)) * DK ** (-0.5)
    key_rows = unit_norm(split_heads(key_rows, head_count))
    value_rows = split_heads(value_rows, head_count)
    beta_rows = jnp.transpose(jax.nn.sigmoid(in_beta)).reshape(head_count, block_count, BLOCK)
    rate_rows = jnp.transpose(-jnp.exp(log_rate)[None, :] * jax.nn.softplus(in_decay + bias_rate[None, :]))
    rate_rows = rate_rows.reshape(head_count, block_count, BLOCK)
    return block_prep(query_rows, key_rows, value_rows, beta_rows, rate_rows, seg_blocks, seg_before)

def run_blocks(solved_keys, solved_values, scores, gamma_in, to_end, gamma_all, query_rows, key_rows, raw_gate, gain_row, state_init):
    head_count, block_count, block_size, value_width = solved_values.shape

    def step(current_state, block_item):
        key_triangular_result, value_triangular_result, score_part, entering_portion, leaving_portion, query_portion, key_portion, complete_portion = block_item
        state_update = value_triangular_result - jnp.einsum('xtl,xln->xtn', key_triangular_result, current_state, precision=exact_precision)
        final_result = entering_portion[..., None] * jnp.einsum('xtl,xln->xtn', query_portion, current_state, precision=exact_precision)
        final_result = final_result + jnp.einsum('hij,hjv->hiv', score_part, state_update, precision=exact_precision)
        following_state = complete_portion[:, None, None] * current_state + jnp.einsum('aqd,aqe->ade', key_portion * leaving_portion[..., None], state_update, precision=exact_precision)
        return (following_state, final_result)
    block_items = tuple((jnp.moveaxis(member, 1, 0) for member in (solved_keys, solved_values, scores, gamma_in, to_end, query_rows, key_rows))) + (jnp.transpose(gamma_all),)
    state_last, outputs = lax.scan(jax.checkpoint(step), state_init, block_items)
    row_count = block_count * block_size
    outputs = jnp.transpose(outputs, (0, 2, 1, 3)).reshape(row_count, head_count, value_width)
    gate_rows = raw_gate.reshape(row_count, head_count, value_width)
    normed = outputs * lax.rsqrt(lax.optimization_barrier(jnp.mean(outputs * outputs, axis=-1, keepdims=True)) + 1e-05) * gain_row * jax.nn.silu(gate_rows)
    return (normed.reshape(row_count, head_count * value_width), state_last)

def layer_forward(weights, token_rows, seg_row):
    first_gain, query_weight, key_weight, value_weight, gate_weight, beta_weight, decay_weight, conv_query, conv_key, conv_value, decay_log, decay_bias, output_gain, out_weight, second_gain, ffn_gate, ffn_up, ffn_down = weights
    hidden_in = low(rms_scale(token_rows, first_gain))
    raw_query = low_back(mult(hidden_in, query_weight))
    raw_key = low_back(mult(hidden_in, key_weight))
    raw_value = low_back(mult(hidden_in, value_weight))
    raw_gate = low_back(mult(hidden_in, gate_weight))
    raw_beta = low_back(mult(hidden_in, beta_weight))
    raw_decay = low_back(mult(hidden_in, decay_weight))
    tail_rows = CONV - 1
    seg_pad = jnp.concatenate([jnp.full((tail_rows,), -1, jnp.int32), seg_row.astype(jnp.int32)])
    seg_blocks = seg_row.reshape(LENGTH // BLOCK, BLOCK)
    seg_before = seg_pad[tail_rows - 1:tail_rows - 1 + LENGTH:BLOCK]
    pad_query = jnp.zeros((tail_rows, raw_query.shape[1]), jnp.float32)
    pad_value = jnp.zeros((tail_rows, raw_value.shape[1]), jnp.float32)
    prepared = mixer_inputs(raw_query, raw_key, raw_value, raw_beta, raw_decay, pad_query, pad_query, pad_value, conv_query, conv_key, conv_value, decay_log, decay_bias, seg_pad, seg_blocks, seg_before)
    state_init = jnp.zeros((decay_log.shape[0], DK, DV), jnp.float32)
    normed, _ = run_blocks(*prepared, raw_gate, output_gain, state_init)
    mixer = low_back(mult(low(normed), out_weight))
    resid = token_rows + mixer
    hidden_mid = low(rms_scale(resid, second_gain))
    gate_pre = low_back(mult(hidden_mid, ffn_gate))
    up_pre = low_back(mult(hidden_mid, ffn_up))
    activated = low(jax.nn.silu(gate_pre) * up_pre)
    return resid + low_back(mult(activated, ffn_down))

def reference(tokens, segments, first_gain, query_weight, key_weight, value_weight, gate_weight, beta_weight, decay_weight, conv_query, conv_key, conv_value, decay_log, decay_bias, output_gain, out_weight, second_gain, ffn_gate, ffn_up, ffn_down, out_grad):
    params = tuple((member.astype(jnp.float32) for member in (first_gain, query_weight, key_weight, value_weight, gate_weight, beta_weight, decay_weight, conv_query, conv_key, conv_value, decay_log, decay_bias, output_gain, out_weight, second_gain, ffn_gate, ffn_up, ffn_down)))
    token_rows = tokens.astype(jnp.float32).reshape(-1, LENGTH, D)
    seg_rows = segments.reshape(-1, LENGTH)

    def forward_all(weights, inputs):

        def one_sequence(seq_pair):
            return layer_forward(weights, seq_pair[0], seq_pair[1])
        return lax.map(jax.checkpoint(one_sequence), (inputs, seg_rows))
    outputs, pull_back = jax.vjp(forward_all, params, token_rows)
    param_grads, input_grad = pull_back(out_grad.astype(jnp.float32).reshape(-1, LENGTH, D))
    layer_out = outputs.astype(jnp.bfloat16).reshape(tokens.shape)
    return (layer_out, input_grad.reshape(tokens.shape), param_grads[0], param_grads[1], param_grads[2], param_grads[3], param_grads[4], param_grads[5], param_grads[6], param_grads[7], param_grads[8], param_grads[9], param_grads[10], param_grads[11], param_grads[12], param_grads[13], param_grads[14], param_grads[15], param_grads[16], param_grads[17])
```

```python
import functools

import jax
import jax.numpy as jnp
from jax import lax
from jax.experimental import pallas as pl
from jax.experimental.pallas import tpu as pltpu
from jax.sharding import PartitionSpec as P

D = 1024
H = 4
DK = 128
DV = 256
CONV = 4
HALO = 16
MESH = pl.DeviceIdType.MESH
EXACT = lax.Precision.HIGHEST
F32 = jnp.float32
BF16 = jnp.bfloat16
DMA = pltpu.SemaphoreType.DMA


def remote(src, dst, sent, got, **device):
    return pltpu.make_async_remote_copy(
        src_ref=src, dst_ref=dst, send_sem=sent, recv_sem=got, device_id=device, device_id_type=MESH
    )


def per_micro(shape):
    zeros = (0,) * (len(shape) - 1)
    return pl.BlockSpec((1,) + tuple(shape[1:]), lambda m: (m,) + zeros)


def fixed(shape):
    zeros = (0,) * len(shape)
    return pl.BlockSpec(tuple(shape), lambda m: zeros)


SCALARS = pl.BlockSpec(memory_space=pltpu.SMEM)
ANYWHERE = pl.BlockSpec(memory_space=pl.ANY)


def shapes_of(outs):
    return [jax.ShapeDtypeStruct(shape, kind) for shape, kind in outs]


class Place:
    def __init__(self, depth):
        self.depth = depth
        self.dp = lax.axis_index("dp")
        self.z = lax.axis_index("ctx")
        self.rank = lax.axis_index("tp")
        x = self.dp % 2
        y = self.dp // 2
        self.x_peer = y * 2 + (1 - x)
        self.y_peer = (1 - y) * 2 + x
        self.diagonal = (1 - y) * 2 + (1 - x)


def signal(**device):
    pl.semaphore_signal(
        pltpu.get_barrier_semaphore(), inc=1, device_id=device, device_id_type=MESH
    )


def greet(place, plane, tensor=False, steep=False):
    z, depth = place.z, place.depth
    others = 0
    each = 2 if steep else 1
    if plane:
        signal(dp=place.x_peer)
        signal(dp=place.y_peer)
        others += 2
    if tensor:
        signal(tp=1 - place.rank)
        others += 1

    @pl.when(z > 0)
    def _():
        signal(ctx=z - 1)
        if steep:
            signal(ctx=z - 1, tp=1 - place.rank)

    @pl.when(z < depth - 1)
    def _():
        signal(ctx=z + 1)
        if steep:
            signal(ctx=z + 1, tp=1 - place.rank)

    return others + each * (jnp.minimum(z, 1) + jnp.minimum(depth - 1 - z, 1))


def greeted(amount):
    pl.semaphore_wait(pltpu.get_barrier_semaphore(), amount)


def line_steps(place, shards, slots, sems):
    (
        local_sem,
        z_send,
        z_recv,
        x_send,
        x_recv,
        y_send,
        y_recv,
        dx_send,
        dx_recv,
        dy_send,
        dy_recv,
    ) = sems
    dp, z, depth = place.dp, place.z, place.depth
    x_peer, y_peer = place.x_peer, place.y_peer
    w_refs = shards
    half = w_refs[0].shape[0] // 2
    count = len(w_refs)

    def slot(a, d, k):
        return slots[a](d * depth + k)

    def x_copy(a, k, src=None):
        src = slot(a, dp, k) if src is None else src
        return remote(src, slot(a, dp, k), x_send.at[a, k], x_recv.at[a, k], dp=x_peer)

    def y_copy(a, k, src=None):
        src = slot(a, dp, k) if src is None else src
        return remote(src, slot(a, dp, k), y_send.at[a, k], y_recv.at[a, k], dp=y_peer)

    def z_copy(a, k, up, src=None):
        src = slot(a, dp, k) if src is None else src
        sent = z_send.at[a, 2 * k + (0 if up else 1)]
        return remote(src, slot(a, dp, k), sent, z_recv.at[a, k], ctx=z + 1 if up else z - 1)

    def top(a, k, d):
        part = slot(a, d, k).at[pl.ds(0, half)]
        return remote(part, part, dy_send.at[a, k], dy_recv.at[a, k], dp=y_peer)

    def bottom(a, k, d):
        part = slot(a, d, k).at[pl.ds(half, half)]
        return remote(part, part, dx_send.at[a, k], dx_recv.at[a, k], dp=x_peer)

    def from_x(a, k):
        part = slot(a, x_peer, k)
        return remote(part, part, x_send.at[a, k], x_recv.at[a, k], dp=x_peer)

    def from_y(a, k):
        part = slot(a, y_peer, k)
        return remote(part, part, y_send.at[a, k], y_recv.at[a, k], dp=y_peer)

    def pass_on(a, k):
        from_x(a, k).wait_recv()
        top(a, k, x_peer).start()
        from_y(a, k).wait_recv()
        bottom(a, k, y_peer).start()

    def keep(a):
        return pltpu.make_async_copy(w_refs[a], slot(a, dp, z), local_sem.at[a])

    def begin():
        for a in range(count):

            @pl.when(z > 0)
            def _(a=a):
                z_copy(a, z, False, w_refs[a]).start()

            @pl.when(z < depth - 1)
            def _(a=a):
                z_copy(a, z, True, w_refs[a]).start()

            x_copy(a, z, w_refs[a]).start()
            y_copy(a, z, w_refs[a]).start()
            keep(a).start()

    def hop(s):
        for a in range(count):

            @pl.when(z >= s)
            def _(a=a):
                k = z - s
                z_copy(a, k, True).wait_recv()

                @pl.when(z < depth - 1)
                def _():
                    z_copy(a, k, True).start()

                x_copy(a, k).start()
                y_copy(a, k).start()

            @pl.when(z + s <= depth - 1)
            def _(a=a):
                k = z + s
                z_copy(a, k, False).wait_recv()

                @pl.when(z > 0)
                def _():
                    z_copy(a, k, False).start()

                x_copy(a, k).start()
                y_copy(a, k).start()

        plane(s - 1)

    def plane(s):
        for a in range(count):
            if s == 0:
                pass_on(a, z)
                continue

            @pl.when(z >= s)
            def _(a=a):
                pass_on(a, z - s)

            @pl.when(z + s <= depth - 1)
            def _(a=a):
                pass_on(a, z + s)

    def finish():
        for a in range(count):
            keep(a).wait()
            for k in range(depth):
                top(a, k, place.diagonal).wait_recv()
                bottom(a, k, place.diagonal).wait_recv()
        for a in range(count):
            for k in range(depth):
                top(a, k, x_peer).wait_send()
                bottom(a, k, y_peer).wait_send()
                x_copy(a, k).wait_send()
                y_copy(a, k).wait_send()

                @pl.when(jnp.logical_and(z < depth - 1, k <= z))
                def _(a=a, k=k):
                    z_copy(a, k, True).wait_send()

                @pl.when(jnp.logical_and(z > 0, k >= z))
                def _(a=a, k=k):
                    z_copy(a, k, False).wait_send()

    hops = [functools.partial(hop, s) for s in range(1, depth)]
    return [begin] + hops + [functools.partial(plane, depth - 1), finish]


def plane_steps(place, shards, slots, sems):
    (
        local_sem,
        z_send,
        z_recv,
        x_send,
        x_recv,
        y_send,
        y_recv,
        dx_send,
        dx_recv,
        dy_send,
        dy_recv,
    ) = sems
    dp, z, depth = place.dp, place.z, place.depth
    x_peer, y_peer = place.x_peer, place.y_peer
    columns_of = [dp, x_peer, y_peer, place.diagonal]
    half = shards[0].shape[0] // 2
    count = len(shards)

    def slot(a, d, k):
        return slots[a](d * depth + k)

    def z_copy(a, c, k, up, src=None):
        part = slot(a, columns_of[c], k)
        sent = z_send.at[a, c, 2 * k + (0 if up else 1)]
        got = z_recv.at[a, c, k]
        return remote(part if src is None else src, part, sent, got, ctx=z + 1 if up else z - 1)

    def to_x(a, d, src):
        return remote(src, slot(a, d, z), x_send.at[a], x_recv.at[a], dp=x_peer)

    def to_y(a, d, src):
        return remote(src, slot(a, d, z), y_send.at[a], y_recv.at[a], dp=y_peer)

    def top(a, d):
        part = slot(a, d, z).at[pl.ds(0, half)]
        return remote(part, part, dy_send.at[a], dy_recv.at[a], dp=y_peer)

    def bottom(a, d):
        part = slot(a, d, z).at[pl.ds(half, half)]
        return remote(part, part, dx_send.at[a], dx_recv.at[a], dp=x_peer)

    def keep(a):
        return pltpu.make_async_copy(shards[a], slot(a, dp, z), local_sem.at[a])

    def leave_plane(a, c, src=None):
        @pl.when(z > 0)
        def _():
            z_copy(a, c, z, False, src).start()

        @pl.when(z < depth - 1)
        def _():
            z_copy(a, c, z, True, src).start()

    def hop(a, c, s):
        @pl.when(z >= s)
        def _():
            z_copy(a, c, z - s, True).wait_recv()

            @pl.when(z < depth - 1)
            def _():
                z_copy(a, c, z - s, True).start()

        @pl.when(z + s <= depth - 1)
        def _():
            z_copy(a, c, z + s, False).wait_recv()

            @pl.when(z > 0)
            def _():
                z_copy(a, c, z + s, False).start()

    def begin():
        for a in range(count):
            to_x(a, dp, shards[a]).start()
            to_y(a, dp, shards[a]).start()
            leave_plane(a, 0, shards[a])
            keep(a).start()

    def across():
        for a in range(count):
            to_x(a, x_peer, slot(a, x_peer, z)).wait_recv()
            top(a, x_peer).start()
            leave_plane(a, 1)
            to_y(a, y_peer, slot(a, y_peer, z)).wait_recv()
            bottom(a, y_peer).start()
            leave_plane(a, 2)

    def hops(s):
        for a in range(count):
            if s == 1:
                top(a, place.diagonal).wait_recv()
                bottom(a, place.diagonal).wait_recv()
                leave_plane(a, 3)
            for c in range(3):
                hop(a, c, s)
            if s > 1:
                hop(a, 3, s - 1)

    def finish():
        for a in range(count):
            hop(a, 3, depth - 1)
            keep(a).wait()
        for a in range(count):
            to_x(a, dp, shards[a]).wait_send()
            to_y(a, dp, shards[a]).wait_send()
            top(a, x_peer).wait_send()
            bottom(a, y_peer).wait_send()
            for c in range(4):
                for k in range(depth):

                    @pl.when(jnp.logical_and(z < depth - 1, k <= z))
                    def _(a=a, c=c, k=k):
                        z_copy(a, c, k, True).wait_send()

                    @pl.when(jnp.logical_and(z > 0, k >= z))
                    def _(a=a, c=c, k=k):
                        z_copy(a, c, k, False).wait_send()

    return [begin, across] + [functools.partial(hops, s) for s in range(1, depth)] + [finish]


def part_of(cols):
    return max(128, round(cols * 2 / 9 / 128) * 128)


def gather_spans(widths):
    left = part_of(sum(widths))
    line, plane = [], []
    for a, width in reversed(list(enumerate(widths))):
        taken = min(left, width)
        left -= taken
        if taken:
            plane.append((a, width - taken, taken))
        if width > taken:
            line.append((a, 0, width - taken))
    return line[::-1], plane[::-1]


def gather_scratch(widths, depth):
    line, plane = (len(part) for part in gather_spans(widths))
    return (
        [DMA((line,)), DMA((line, 2 * depth))]
        + [DMA((line, depth))] * 9
        + [DMA((plane,)), DMA((plane, 4, 2 * depth)), DMA((plane, 4, depth))]
        + [DMA((plane,))] * 8
    )


def gather_steps(place, w_refs, out_refs, sems):
    line, plane = gather_spans([ref.shape[1] for ref in w_refs])

    def views(spans):
        shards = [w_refs[a].at[:, pl.ds(start, width)] for a, start, width in spans]

        def slot(a, start, width, k):
            return out_refs[a].at[k, :, pl.ds(start, width)]

        return shards, [functools.partial(slot, *span) for span in spans]

    first = line_steps(place, *views(line), sems[:11])
    second = plane_steps(place, *views(plane), sems[11:])

    def both(p, q):
        p()
        q()

    return [functools.partial(both, p, q) for p, q in zip(first, second)]


def scatter_scratch(widths, rows, depth):
    cols = sum(widths)
    whole = pltpu.VMEM((depth, rows, cols), BF16)
    part = pltpu.VMEM((depth, rows // 2, cols), BF16)
    return (
        [pltpu.VMEM((4 * depth, rows, cols), BF16), part, part, whole, whole]
        + [pltpu.VMEM((depth + 1, rows, cols), BF16)]
        + [DMA((4 * len(widths),))]
        + [DMA((depth,))] * 12
    )


def scatter_steps(place, g_refs, out_ref, scratch):
    (
        g,
        from_dx,
        from_dy,
        from_x,
        from_y,
        from_line,
        load,
        dx_send,
        dx_recv,
        dy_send,
        dy_recv,
        x_send,
        x_recv,
        y_send,
        y_recv,
        up_send,
        up_recv,
        down_send,
        down_recv,
    ) = scratch
    n = len(g_refs)
    widths = [ref.shape[2] for ref in g_refs]
    dp, z, depth = place.dp, place.z, place.depth
    x_peer, y_peer, diagonal = place.x_peer, place.y_peer, place.diagonal
    rows, cols = out_ref.shape
    half = rows // 2
    starts = [sum(widths[:i]) for i in range(n)]

    def loads(stage, column):
        return [
            pltpu.make_async_copy(
                g_refs[i].at[pl.ds(column * depth, depth)],
                g.at[pl.ds(column * depth, depth), :, pl.ds(starts[i], widths[i])],
                load.at[stage * n + i],
            )
            for i in range(n)
        ]

    stages = [loads(0, diagonal), loads(1, x_peer), loads(2, y_peer), loads(3, dp)]

    def block_at(i):
        tables = [
            sorted(range(depth), key=lambda k: (-abs(k - zz), -k if 2 * zz < depth else k))[i]
            for zz in range(depth)
        ]
        k = tables[0]
        for zz in range(1, depth):
            k = jnp.where(z == zz, tables[zz], k)
        return k

    order = [block_at(i) for i in range(depth)]

    def to_y(k):
        src = g.at[diagonal * depth + k, pl.ds(0, half)]
        return remote(src, from_dy.at[k], dy_send.at[k], dy_recv.at[k], dp=y_peer)

    def to_x(k):
        src = g.at[diagonal * depth + k, pl.ds(half, half)]
        return remote(src, from_dx.at[k], dx_send.at[k], dx_recv.at[k], dp=x_peer)

    def full_x(k):
        src = g.at[x_peer * depth + k]
        return remote(src, from_x.at[k], x_send.at[k], x_recv.at[k], dp=x_peer)

    def full_y(k):
        src = g.at[y_peer * depth + k]
        return remote(src, from_y.at[k], y_send.at[k], y_recv.at[k], dp=y_peer)

    def up(k):
        src = g.at[dp * depth + k]
        return remote(src, from_line.at[k + 1], up_send.at[k], up_recv.at[k], ctx=z + 1)

    def down(k):
        src = g.at[dp * depth + k]
        return remote(src, from_line.at[k], down_send.at[k], down_recv.at[k], ctx=z - 1)

    def each(row_count, body):
        def turn(i, carry):
            body(pl.multiple_of(i * 16, 16))
            return carry

        lax.fori_loop(0, row_count // 16, turn, 0)

    def add_diagonal(k):
        a = x_peer * depth + k
        b = y_peer * depth + k

        def body(row):
            rows = pl.ds(row, 16)
            others = pl.ds(row + half, 16)
            g[a, rows] = (g[a, rows].astype(F32) + from_dy[k, rows].astype(F32)).astype(BF16)
            g[b, others] = (g[b, others].astype(F32) + from_dx[k, rows].astype(F32)).astype(BF16)

        each(half, body)

    def add_full(k):
        a = dp * depth + k

        def body(row):
            rows = pl.ds(row, 16)
            total = g[a, rows].astype(F32) + from_x[k, rows].astype(F32)
            g[a, rows] = (total + from_y[k, rows].astype(F32)).astype(BF16)

        each(2 * half, body)

    def add_line(k, at):
        a = dp * depth + k

        def body(row):
            rows = pl.ds(row, 16)
            g[a, rows] = (g[a, rows].astype(F32) + from_line[at, rows].astype(F32)).astype(BF16)

        each(2 * half, body)

    def start_diagonal(i):
        to_y(order[i]).start()
        to_x(order[i]).start()

    def send_line(k):
        @pl.when(k > z)
        def _():
            @pl.when(z > 0)
            def _():
                up(k).wait_recv()
                add_line(k, k + 1)

            up(k).start()

        @pl.when(k < z)
        def _():
            @pl.when(z < depth - 1)
            def _():
                down(k).wait_recv()
                add_line(k, k)

            down(k).start()

    def plane_done(k):
        full_x(k).wait_recv()
        full_y(k).wait_recv()
        add_full(k)

    def load_all():
        for stage in stages:
            for copy in stage:
                copy.start()

    def begin():
        for copy in stages[0]:
            copy.wait()
        for i in range(min(2, depth)):
            start_diagonal(i)
        for copy in stages[1] + stages[2]:
            copy.wait()

    def block(i):
        k = order[i]
        to_y(k).wait_recv()
        to_x(k).wait_recv()
        add_diagonal(k)
        full_x(k).start()
        full_y(k).start()
        if i + 2 < depth:
            start_diagonal(i + 2)
        if i == 0:
            for copy in stages[3]:
                copy.wait()
        if i >= 1:
            plane_done(order[i - 1])
        if i >= 2:
            send_line(order[i - 2])

    def last_lines():
        plane_done(order[depth - 1])
        for i in range(max(depth - 2, 0), depth - 1):
            send_line(order[i])

    def finish():
        @pl.when(z > 0)
        def _():
            up(z).wait_recv()

        @pl.when(z < depth - 1)
        def _():
            down(z).wait_recv()

        def total(row):
            rows = pl.ds(row, 16)
            value = g[dp * depth + z, rows].astype(F32)
            value = value + jnp.where(z > 0, from_line[z + 1, rows].astype(F32), 0.0)
            out_ref[rows] = value + jnp.where(z < depth - 1, from_line[z, rows].astype(F32), 0.0)

        each(2 * half, total)
        for k in range(depth):
            to_y(k).wait_send()
            to_x(k).wait_send()
            full_x(k).wait_send()
            full_y(k).wait_send()

            @pl.when(k > z)
            def _(k=k):
                up(k).wait_send()

            @pl.when(k < z)
            def _(k=k):
                down(k).wait_send()

    return load_all, [begin] + [functools.partial(block, i) for i in range(depth)] + [last_lines, finish]


def swap_kernel(mine_ref, theirs_ref, sent, got):
    peer = 1 - lax.axis_index("tp")
    barrier = pltpu.get_barrier_semaphore()
    pl.semaphore_signal(barrier, inc=1, device_id={"tp": peer}, device_id_type=MESH)
    pl.semaphore_wait(barrier, 1)
    copy = remote(mine_ref, theirs_ref, sent, got, tp=peer)
    copy.start()
    copy.wait()


def swap(mine, collective):
    return pl.pallas_call(
        swap_kernel,
        out_shape=jax.ShapeDtypeStruct(mine.shape, mine.dtype),
        in_specs=[pl.BlockSpec(memory_space=pl.ANY)],
        out_specs=pl.BlockSpec(memory_space=pl.ANY),
        scratch_shapes=[DMA, DMA],
        compiler_params=pltpu.CompilerParams(collective_id=collective, has_side_effects=True),
    )(mine)


def entry_kernel(depth, count, *refs):
    token_ref, w_refs, refs = refs[0], refs[1 : 1 + count], refs[1 + count :]
    block_ref, refs = refs[0], refs[1:]
    full_refs, refs = refs[: min(count, 1)], refs[min(count, 1) :]
    keep, sent, got, tail_sent, tail_got = refs[:5]
    place = Place(depth)
    z, rank = place.z, place.rank
    micro, n, width = token_ref.shape

    def mine(first, rows):
        at = pl.ds(pl.multiple_of(rank * width, 128), width)
        return block_ref.at[:, pl.ds(first, rows), at]

    own = pltpu.make_async_copy(token_ref, mine(HALO, n), keep.at[0])
    other = remote(token_ref, mine(HALO, n), sent, got, tp=1 - rank)
    last = token_ref.at[:, pl.ds(n - HALO, HALO)]
    start = token_ref.at[:, pl.ds(0, HALO)]

    def tails(src, **device):
        return [
            remote(src, mine(0, HALO), tail_sent.at[i], tail_got.at[rank], tp=t, **device)
            for i, t in enumerate((rank, 1 - rank))
        ]

    spare = pltpu.make_async_copy(start, mine(0, HALO), keep.at[1])
    spare_other = remote(start, mine(0, HALO), tail_sent.at[1], tail_got.at[rank], tp=1 - rank)
    if count:
        shard_ref, load, refs = refs[5], refs[6], refs[7:]
        loads, at = [], 0
        for i, ref in enumerate(w_refs):
            columns_at = pl.ds(at, ref.shape[1])
            loads.append(pltpu.make_async_copy(ref, shard_ref.at[:, columns_at], load.at[i]))
            at += ref.shape[1]
        for copy in loads:
            copy.start()
    own.start()
    greeted(greet(place, count > 0, tensor=True, steep=True))
    if count:
        steps = gather_steps(place, [shard_ref], full_refs, refs)
        for copy in loads:
            copy.wait()
        steps[0]()
    other.start()

    @pl.when(z < depth - 1)
    def _():
        for copy in tails(last, ctx=z + 1):
            copy.start()

    @pl.when(z == 0)
    def _():
        spare.start()
        spare_other.start()

    if count:
        for step in steps[1:]:
            step()
    own.wait()
    other.wait()

    @pl.when(z == 0)
    def _():
        spare.wait()
        spare_other.wait_send()
        remote(start, mine(0, HALO), tail_sent.at[1], tail_got.at[1 - rank], tp=1 - rank).wait_recv()

    @pl.when(z > 0)
    def _():
        for t in range(2):
            remote(last, mine(0, HALO), tail_sent.at[0], tail_got.at[t], tp=1 - rank).wait_recv()

    @pl.when(z < depth - 1)
    def _():
        for copy in tails(last, ctx=z + 1):
            copy.wait_send()


def entry(tokens, shards, collective):
    micro, n, width = tokens.shape
    depth = lax.axis_size("ctx")
    count = len(shards)
    block = jax.ShapeDtypeStruct((micro, HALO + n, 2 * width), BF16)
    scratch = [DMA((2,)), DMA, DMA, DMA((2,)), DMA((2,))]
    full = []
    if count:
        rows, cols = shards[0].shape[0], sum(w.shape[1] for w in shards)
        full = [jax.ShapeDtypeStruct((4 * depth, rows, cols), BF16)]
        scratch += [pltpu.VMEM((rows, cols), BF16), DMA((count,))] + gather_scratch([cols], depth)
    return pl.pallas_call(
        functools.partial(entry_kernel, depth, count),
        in_specs=[ANYWHERE] * (1 + count),
        out_specs=[ANYWHERE] * (1 + len(full)),
        out_shape=[block] + full,
        scratch_shapes=scratch,
        compiler_params=pltpu.CompilerParams(collective_id=collective, has_side_effects=True),
    )(tokens, *shards)


def total_peers(sizes):
    for axis, size in sizes:
        place = lax.axis_index(axis)
        bit = 1
        while bit < size:
            yield axis, place + bit - 2 * bit * ((place // bit) % 2)
            bit *= 2


def exit_kernel(depth, sizes, count, *refs):
    part_ref, block_ref, resid_ref, gain_ref, second_ref, taps_ref, decay_ref, norm_ref = refs[:8]
    g_refs, refs = refs[8 : 8 + count], refs[8 + count :]
    token_ref, total_ref, refs = refs[0], refs[1], refs[2:]
    sum_refs, refs = refs[: min(count, 1)], refs[min(count, 1) :]
    theirs, front, arrived, rows_buf, sent, got, front_sent, front_got, add_sent, add_got = refs[:10]
    refs = refs[10:]
    place = Place(depth)
    z, rank = place.z, place.rank
    micro, rows, features = part_ref.shape
    n, width = rows - HALO, token_ref.shape[2]
    if count:
        load_all, steps = scatter_steps(place, g_refs, sum_refs[0], refs)
        load_all()
    peers = list(total_peers(sizes))
    waiting = greet(place, count > 0, tensor=True, steep=True)
    for axis, peer in peers:
        signal(**{axis: peer})
    greeted(waiting + len(peers))
    swap = remote(part_ref, theirs, sent, got, tp=1 - rank)
    swap.start()
    head = part_ref.at[:, pl.ds(0, HALO)]

    def fronts():
        return [
            remote(head, front.at[rank], front_sent.at[i], front_got.at[rank], ctx=z - 1, tp=t)
            for i, t in enumerate((rank, 1 - rank))
        ]

    @pl.when(z > 0)
    def _():
        for copy in fronts():
            copy.start()

    if count:
        steps[0]()
        steps[1]()
    swap.wait()

    @pl.when(z < depth - 1)
    def _():
        for t in range(2):
            remote(head, front.at[t], front_sent.at[0], front_got.at[t], ctx=z - 1).wait_recv()

    @pl.when(z == depth - 1)
    def _():
        front[...] = jnp.zeros(front.shape, BF16)

    gain = gain_ref[...]
    total = jnp.zeros((1, features), F32)
    for m in range(micro):
        grad = part_ref[m, HALO:].astype(F32) + theirs[m, HALO:].astype(F32)
        tail = front[0, m].astype(F32) + front[1, m].astype(F32)
        grad = jnp.concatenate([grad[: n - HALO], grad[n - HALO :] + tail], axis=0)
        values = block_ref[m, HALO:].astype(F32)
        scale = inverse_root(jnp.mean(values * values, axis=1, keepdims=True) + 1e-06)
        unit = values * scale
        total = total + jnp.sum(grad * unit, axis=0, keepdims=True)
        grad = grad * gain
        moved = scale * (grad - unit * jnp.mean(grad * unit, axis=1, keepdims=True))
        rows_buf[...] = resid_ref[m] + moved
        token_ref[m] = rows_buf[:, pl.ds(pl.multiple_of(rank * width, 128), width)]
    lanes = lax.broadcasted_iota(jnp.int32, (1, features), 1)
    owned = (lanes >= rank * width) & (lanes < (rank + 1) * width)
    total_ref[...] = jnp.zeros_like(total_ref)
    total_ref[0:1] = jnp.where(owned, total, 0.0)
    total_ref[1:2] = jnp.where(owned, second_ref[...], 0.0)
    keys, values = taps_ref.shape[1] // 4, taps_ref.shape[1] // 2

    def lanes_at(start, size):
        return pl.ds(pl.multiple_of(start + rank * size, 128), size)

    total_ref[2:6, lanes_at(0, keys)] = taps_ref[:, :keys]
    total_ref[2:6, lanes_at(2 * keys, keys)] = taps_ref[:, keys : 2 * keys]
    total_ref[6:10, lanes_at(0, values)] = taps_ref[:, 2 * keys :]
    total_ref[10:11, : norm_ref.shape[1]] = norm_ref[...]
    total_ref[11:13, lanes_at(0, 128)] = decay_ref[0:2]
    inner = list(steps[2:]) if count else []
    for i, (axis, peer) in enumerate(peers):
        copy = remote(total_ref, arrived.at[i], add_sent.at[i], add_got.at[i], **{axis: peer})
        copy.start()
        if inner:
            inner.pop(0)()
        copy.wait()
        total_ref[...] += arrived[i]
    for step in inner:
        step()

    @pl.when(z > 0)
    def _():
        for copy in fronts():
            copy.wait_send()


def leave(part, block, resid, gain, smalls, grads, collective):
    micro, rows, features = part.shape
    n = rows - HALO
    depth = lax.axis_size("ctx")
    sizes = tuple((axis, lax.axis_size(axis)) for axis in ("tp", "dp", "ctx"))
    steps = sum(size.bit_length() - 1 for _, size in sizes)
    count = len(grads)
    inside = pl.BlockSpec(memory_space=pltpu.VMEM)
    small = (16, features)
    outs = [((micro, n, features // 2), F32), (small, F32)]
    scratch = [
        pltpu.VMEM(part.shape, BF16),
        pltpu.VMEM((2, micro, HALO, features), BF16),
        pltpu.VMEM((steps,) + small, F32),
        pltpu.VMEM((n, features), F32),
        DMA,
        DMA,
        DMA((2,)),
        DMA((2,)),
        DMA((steps,)),
        DMA((steps,)),
    ]
    if count:
        widths = [a.shape[2] for a in grads]
        outs = outs + [((grads[0].shape[1], sum(widths)), F32)]
        scratch = scratch + scatter_scratch(widths, grads[0].shape[1], depth)
    return pl.pallas_call(
        functools.partial(exit_kernel, depth, sizes, count),
        in_specs=[inside] * 8 + [ANYWHERE] * count,
        out_specs=[inside] * len(outs),
        out_shape=shapes_of(outs),
        scratch_shapes=scratch,
        compiler_params=pltpu.CompilerParams(
            collective_id=collective, has_side_effects=True, vmem_limit_bytes=60 * 2**20
        ),
    )(part, block, resid, gain, *smalls, *grads)


def halves(a):
    high = a.astype(BF16)
    return high, (a - high.astype(F32)).astype(BF16)


def mm(a, b, ca=1, cb=0, exact=True):
    dims = (((ca,), (cb,)), ((), ()))
    if exact:
        return lax.dot_general(a, b, dims, precision=EXACT, preferred_element_type=F32)
    (a_high, a_low), (b_high, b_low) = halves(a), halves(b)

    def part(p, q):
        return lax.dot_general(p, q, dims, preferred_element_type=F32)

    return part(a_high, b_high) + (part(a_high, b_low) + part(a_low, b_high))


def row_sum(a):
    return jnp.sum(a, axis=1, keepdims=True)


def pick(block, lane):
    lanes = lax.broadcasted_iota(jnp.int32, block.shape, 1)
    return row_sum(jnp.where(lanes == lane, block, 0.0))


def iotas(n):
    return (
        lax.broadcasted_iota(jnp.int32, (n, n), 0),
        lax.broadcasted_iota(jnp.int32, (n, n), 1),
    )


def same_masks(seg_col):
    here = seg_col[HALO:]
    return [
        (pltpu.roll(seg_col, lag, 0)[HALO:] == here).astype(F32) if lag else None
        for lag in range(CONV)
    ]


def wide(mask, columns):
    return mask if columns == mask.shape[1] else jnp.concatenate([mask] * (columns // 128), axis=1)


def conv_forward(raw, taps, same):
    total = taps[0:1] * raw[HALO:]
    for lag in range(1, CONV):
        total = total + taps[lag : lag + 1] * (
            pltpu.roll(raw, lag, 0)[HALO:] * wide(same[lag], raw.shape[1])
        )
    return total


def conv_backward(raw, taps, same, grad):
    rows, columns = raw.shape
    empty = jnp.zeros((HALO, columns), F32)
    tap_grads = [jnp.sum(grad * raw[HALO:], axis=0, keepdims=True)]
    total = jnp.concatenate([empty, taps[0:1] * grad], axis=0)
    for lag in range(1, CONV):
        kept = grad * wide(same[lag], columns)
        tap_grads.append(jnp.sum(kept * pltpu.roll(raw, lag, 0)[HALO:], axis=0, keepdims=True))
        total = total + pltpu.roll(
            jnp.concatenate([empty, taps[lag : lag + 1] * kept], axis=0), rows - lag, 0
        )
    return total, jnp.concatenate(tap_grads, axis=0)


def inverse_root(v):
    root = lax.rsqrt(v)
    return root * (1.5 - 0.5 * v * root * root)


def sigmoid(v):
    return 1.0 / (1.0 + jnp.exp(-v))


def softplus(v):
    return jnp.maximum(v, 0.0) + jnp.log(1.0 + jnp.exp(-jnp.abs(v)))


def unit_inverse(strict):
    n = strict[0].shape[0]
    if n > 128 and n % 256 == 0:
        half = n // 2
        corners = unit_inverse([a[:half, :half] for a in strict] + [a[half:, half:] for a in strict])
        first, second = corners[: len(strict)], corners[len(strict) :]
        low = [mm(a[half:, :half], p) for a, p in zip(strict, first)]
        low = [mm(q, a) for q, a in zip(second, low)]
        empty = jnp.zeros((half, half), F32)
        return [
            jnp.concatenate(
                [jnp.concatenate([p, empty], axis=1), jnp.concatenate([-a, q], axis=1)], axis=0
            )
            for p, q, a in zip(first, second, low)
        ]
    r, c = iotas(n)
    inverse = [jnp.where(r == c, 1.0, 0.0)] * len(strict)
    size = 1
    while size < n:
        mask = (r // (2 * size) == c // (2 * size)) & (r // size > c // size)
        parts = [jnp.where(mask, a, 0.0) for a in strict]
        if size > 1:
            parts = [mm(part, a) for part, a in zip(parts, inverse)]
            parts = [mm(a, part) for part, a in zip(parts, inverse)]
        inverse = [a - part for part, a in zip(parts, inverse)]
        size *= 2
    return inverse


def two_sum(a, b):
    total = a + b
    part = total - a
    return total, (a - (total - part)) + (b - part)


def running_sums(rates):
    n = rates.shape[0]
    r, c = iotas(n)
    inside = mm(((r >= c) & (r // 64 == c // 64)).astype(F32), rates, exact=True)
    high = low = jnp.zeros((1, rates.shape[1]), F32)
    highs, lows = [], []
    for start in range(0, n, 64):
        rows = inside[start : start + 64]
        total, error = two_sum(high, rows)
        highs.append(total)
        lows.append(error + low)
        high, error = two_sum(high, rows[63:64])
        low = low + error
    return jnp.concatenate(highs, axis=0), jnp.concatenate(lows, axis=0)


def decay_terms(rates, seg_col, seg_row, heads):
    n = rates.shape[0]
    r, c = iotas(n)
    highs, lows = running_sums(rates)
    high_rows, low_rows = jnp.transpose(highs), jnp.transpose(lows)
    here = seg_col[HALO:, 0:1]
    before = seg_col[HALO - 1 : HALO, 0:1]
    end = seg_col[HALO + n - 1 : HALO + n, 0:1]
    visible = (r >= c) & (here == seg_row[0:1])
    terms = []
    for head in range(heads):
        lane = heads + head
        high, low = pick(highs, lane), pick(lows, lane)
        ratio = (high - high_rows[lane : lane + 1]) + (low - low_rows[lane : lane + 1])
        decay = jnp.where(visible, jnp.exp(jnp.where(visible, ratio, 0.0)), 0.0)
        last_high, last_low = high[n - 1 : n], low[n - 1 : n]
        gamma_in = jnp.exp(high + low) * (here == before).astype(F32)
        to_end = jnp.exp((last_high - high) + (last_low - low)) * (here == end).astype(F32)
        gamma_all = jnp.exp(last_high + last_low) * (end == before).astype(F32)
        terms.append((decay, gamma_in, to_end, gamma_all))
    return terms


def rate_block(small, log_ref, bias_ref, heads):
    lanes = lax.broadcasted_iota(jnp.int32, small.shape, 1)
    rates = jnp.zeros(small.shape, F32)
    slopes = jnp.zeros(small.shape, F32)
    for head in range(heads):
        shifted = small + bias_ref[head]
        factor = -jnp.exp(jnp.full((1, 1), log_ref[head], F32))
        rates = jnp.where(lanes == heads + head, factor * softplus(shifted), rates)
        slopes = jnp.where(lanes == heads + head, factor * sigmoid(shifted), slopes)
    return rates, slopes


def head_rows(raw, taps, same, normal):
    mixed = conv_forward(raw, taps, same)
    rows = mixed * sigmoid(mixed)
    if not normal:
        return mixed, rows, None
    return mixed, rows, inverse_root(row_sum(rows * rows) + 1e-06)


def columns(ref, start, width):
    return ref[0, :, start : start + width]


def project(hidden, full_ref, raw_ref, cuts):
    for start, end in zip(cuts[:-1], cuts[1:]):
        raw_ref[0, :, start:end] = jnp.dot(
            hidden, full_ref[:, start:end], preferred_element_type=F32
        )


def cuts_of(heads):
    keys, values = heads * DK, heads * DV
    gate = 2 * keys + values
    return [0, keys, 2 * keys, gate, gate + values, gate + values + 128]


def state_scratch(units):
    return [
        pltpu.VMEM((units, DK, DV), F32),
        pltpu.VMEM((units, DK, DV), F32),
        DMA((units,)),
        DMA((units,)),
    ]


def state_copy(place, up, scratch, unit):
    out_buf, in_buf, sent, got = scratch
    target = place.z + 1 if up else place.z - 1
    return remote(out_buf.at[unit], in_buf.at[unit], sent.at[unit], got.at[unit], ctx=target)


def state_line(place, up, scratch, unit):
    out_buf, in_buf, _, _ = scratch
    z, depth = place.z, place.depth
    first, last = (0, depth - 1) if up else (depth - 1, 0)
    copy = state_copy(place, up, scratch, unit)

    def receive():
        @pl.when(z == first)
        def _():
            in_buf[unit] = jnp.zeros(in_buf.shape[1:], F32)

        @pl.when(z != first)
        def _():
            copy.wait_recv()

        return in_buf[unit]

    def send(value):
        @pl.when(z != last)
        def _():
            out_buf[unit] = value()
            copy.start()

    return receive, send


def state_sent(place, up, scratch, units):
    @pl.when(place.z != (place.depth - 1 if up else 0))
    def _():
        for unit in range(units):
            state_copy(place, up, scratch, unit).wait_send()


def at_turn(i, step):
    @pl.when(pl.program_id(0) == i)
    def _():
        step()


def between(turn, first, last):
    return jnp.logical_and(turn >= first, turn <= last)


def forward_kernel(heads, depth, micro, count, *refs):
    (
        block_ref,
        seg_col_ref,
        seg_row_ref,
        in_gain_ref,
        in_ref,
        taps_ref,
        gain_ref,
        log_ref,
        bias_ref,
    ) = refs[:9]
    w_refs, refs = refs[9 : 9 + count], refs[9 + count :]
    (
        inverse_ref,
        scores_ref,
        keys_ref,
        values_ref,
        enter_ref,
        move_ref,
        state_ref,
        update_ref,
        mixed_ref,
        normed_ref,
        hidden_ref,
        raw_ref,
    ) = refs[:12]
    full_refs, refs = refs[12 : 12 + count], refs[12 + count :]
    kept_gate, kept_scores, kept_keys, kept_values, kept_enter, kept_moves, kept_adds = refs[:7]
    line, refs = refs[7:11], refs[11:]
    place = Place(depth)
    turn = pl.program_id(0)
    steps = gather_steps(place, w_refs, full_refs, refs) if count else []

    @pl.when(turn == 0)
    def _():
        greeted(greet(place, count > 0))
        for step in steps[:1]:
            step()

    keys, values = heads * DK, heads * DV
    n = keys_ref.shape[2]
    each = range(heads)

    @pl.when(turn < micro)
    def _():
        block = block_ref[0].astype(F32)
        scale = inverse_root(jnp.mean(block * block, axis=1, keepdims=True) + 1e-06)
        hidden = (block * scale * in_gain_ref[...]).astype(BF16)
        hidden_ref[0] = hidden
        project(hidden, in_ref, raw_ref, cuts_of(heads))
        kept_gate[turn] = columns(raw_ref, 2 * keys + values, values)[HALO:]
        seg_col, seg_row = seg_col_ref[0], seg_row_ref[0]
        same = same_masks(seg_col)
        small = columns(raw_ref, 2 * keys + 2 * values, 128)[HALO:]
        rates, _ = rate_block(small, log_ref, bias_ref, heads)
        r, c = iotas(n)
        square = iotas(DK)
        query, key, value = [], [], []
        for head in each:
            at = head * DK
            _, rows, scale = head_rows(
                columns(raw_ref, at, DK), taps_ref[:, at : at + DK], same, True
            )
            query.append(rows * scale * DK ** (-0.5))
            at = keys + head * DK
            _, rows, scale = head_rows(
                columns(raw_ref, at, DK), taps_ref[:, at : at + DK], same, True
            )
            key.append(rows * scale)
            at = 2 * keys + head * DV
            _, rows, _ = head_rows(columns(raw_ref, at, DV), taps_ref[:, at : at + DV], same, False)
            value.append(rows)
        beta = [sigmoid(pick(small, head)) for head in each]
        decay, gamma_in, to_end, gamma_all = zip(*decay_terms(rates, seg_col, seg_row, heads))
        strict = [
            jnp.where(r > c, beta[h] * decay[h] * mm(key[h], key[h], 1, 1), 0.0) for h in each
        ]
        scores = [mm(query[h], key[h], 1, 1) * decay[h] for h in each]
        for i, step in enumerate(steps[1:-1]):
            at_turn(min(i, micro - 1), step)
        inverse = unit_inverse(strict)
        solved_keys = [mm(inverse[h], (beta[h] * gamma_in[h]) * key[h]) for h in each]
        solved_values = [mm(inverse[h], beta[h] * value[h]) for h in each]
        for h in each:
            unit = turn * heads + h
            weighted = key[h] * to_end[h]
            enter = gamma_in[h] * query[h]
            moves = jnp.where(square[0] == square[1], gamma_all[h], 0.0) - mm(
                weighted, solved_keys[h], 0, 0
            )
            inverse_ref[0, h] = inverse[h]
            scores_ref[0, h] = scores[h]
            keys_ref[0, h] = solved_keys[h]
            values_ref[0, h] = solved_values[h]
            enter_ref[0, h] = enter
            move_ref[0, h] = moves
            kept_scores[unit] = scores[h]
            kept_keys[unit] = solved_keys[h]
            kept_values[unit] = solved_values[h]
            kept_enter[unit] = enter
            kept_moves[unit] = moves
            kept_adds[unit] = mm(weighted, solved_values[h], 0, 0)

    @pl.when(turn >= micro)
    def _():
        for h in each:
            unit = (turn - micro) * heads + h
            state = line[1][unit]
            update = kept_values[unit] - mm(kept_keys[unit], state)
            mixed = mm(kept_enter[unit], state) + mm(kept_scores[unit], update)
            state_ref[0, h] = state
            update_ref[0, h] = update
            mixed_ref[0, h] = mixed
            at = h * DV
            gate = kept_gate[turn - micro, :, at : at + DV]
            scale = inverse_root(jnp.mean(mixed * mixed, axis=1, keepdims=True) + 1e-05)
            normed = mixed * scale * gain_ref[...] * (gate * sigmoid(gate))
            normed_ref[0, :, at : at + DV] = normed.astype(BF16)

    reached = turn - place.z

    @pl.when(between(reached, 0, micro - 1))
    def _():
        for h in each:
            unit = reached * heads + h
            receive, send = state_line(place, True, line, unit)
            state = receive()
            send(lambda: mm(kept_moves[unit], state) + kept_adds[unit])

    @pl.when(turn == 2 * micro - 1)
    def _():
        state_sent(place, True, line, micro * heads)
        for step in steps[-1:]:
            step()


def unit_backward(rows, scale, factor, grad):
    return factor * scale * (grad - rows * (scale * scale * row_sum(rows * grad)))


def silu_backward(mixed, grad):
    slope = sigmoid(mixed)
    return grad * slope * (1.0 + mixed * (1.0 - slope))


def scatter_turns(micro, count):
    return [min(2 * i + 1 if i < 2 else micro + i - 2, 2 * micro - 1) for i in range(count)]


def backward_kernel(heads, depth, micro, count, *refs):
    (
        grad_ref,
        mixed_ref,
        gate_ref,
        early_scores_ref,
        early_keys_ref,
        enter_ref,
        move_ref,
        seg_col_ref,
        seg_row_ref,
        inverse_ref,
        scores_ref,
        keys_ref,
        values_ref,
        update_ref,
        state_ref,
        raw_ref,
        in_ref,
        taps_ref,
        gain_ref,
        log_ref,
        bias_ref,
    ) = refs[:21]
    g_refs, refs = refs[21 : 21 + count], refs[21 + count :]
    part_ref, grad_raw_ref, grad_taps_ref, grad_small_ref, grad_gain_ref = refs[:5]
    sum_refs, refs = refs[5 : 5 + (count > 0)], refs[5 + (count > 0) :]
    kept_gate, kept_mixed, kept_update, kept_local = refs[:4]
    line, refs = refs[4:8], refs[8:]
    place = Place(depth)
    turn = pl.program_id(0)
    steps = []
    if count:
        load_all, steps = scatter_steps(place, g_refs, sum_refs[0], refs)

    @pl.when(turn == 0)
    def _():
        if count:
            load_all()
        greeted(greet(place, count > 0))
        for step in steps[:1]:
            step()
        grad_taps_ref[...] = jnp.zeros_like(grad_taps_ref)
        grad_small_ref[...] = jnp.zeros_like(grad_small_ref)
        grad_gain_ref[...] = jnp.zeros_like(grad_gain_ref)

    keys, values = heads * DK, heads * DV
    at_gate = 2 * keys + values
    at_small = at_gate + values
    n = keys_ref.shape[2]

    @pl.when(turn < micro)
    def _():
        for head in range(heads):
            unit_at = turn * heads + head
            at = head * DV
            grad = grad_ref[0, :, at : at + DV]
            mixed = mixed_ref[0, head]
            gate = gate_ref[0, HALO:, at : at + DV]
            slope = sigmoid(gate)
            active = gate * slope
            scale = inverse_root(jnp.mean(mixed * mixed, axis=1, keepdims=True) + 1e-05)
            unit = mixed * scale
            grad_gain_ref[...] += jnp.sum(grad * unit * active, axis=0, keepdims=True)
            grad_gate = grad * unit * gain_ref[...] * slope * (1.0 + gate * (1.0 - slope))
            kept_gate[turn, :, at : at + DV] = grad_gate.astype(BF16)
            grad = grad * active * gain_ref[...]
            grad_mixed = scale * (grad - unit * jnp.mean(grad * unit, axis=1, keepdims=True))
            grad_update = mm(early_scores_ref[0, head], grad_mixed, 0, 0)
            kept_mixed[unit_at] = grad_mixed
            kept_update[unit_at] = grad_update
            kept_local[unit_at] = mm(enter_ref[0, head], grad_mixed, 0, 0) - mm(
                early_keys_ref[0, head], grad_update, 0, 0
            )

    @pl.when(turn >= micro)
    def _():
        m = turn - micro
        grad_raw_ref[0, :HALO, at_gate:at_small] = jnp.zeros((HALO, values), BF16)
        grad_raw_ref[0, HALO:, at_gate:at_small] = kept_gate[m]
        seg_col, seg_row = seg_col_ref[0], seg_row_ref[0]
        same = same_masks(seg_col)
        small = columns(raw_ref, 2 * keys + 2 * values, 128)[HALO:]
        rates, slopes = rate_block(small, log_ref, bias_ref, heads)
        r, c = iotas(n)
        lanes = lax.broadcasted_iota(jnp.int32, (n, 128), 1)
        small_grad = jnp.zeros((n, 128), F32)
        cum_grad = jnp.zeros((n, 128), F32)
        end_grad = jnp.zeros((1, 128), F32)
        terms = decay_terms(rates, seg_col, seg_row, heads)

        def finish(at, width, grad):
            raw = columns(raw_ref, at, width)
            grad_raw, grad_taps = conv_backward(raw, taps_ref[:, at : at + width], same, grad)
            grad_raw_ref[0, :, at : at + width] = grad_raw.astype(BF16)
            grad_taps_ref[:, at : at + width] += grad_taps

        for head in range(heads):
            decay, gamma_in, to_end, gamma_all = terms[head]
            at_query, at_key, at_value = head * DK, keys + head * DK, 2 * keys + head * DV
            mixed_query, rows_query, scale_query = head_rows(
                columns(raw_ref, at_query, DK), taps_ref[:, at_query : at_query + DK], same, True
            )
            query = rows_query * scale_query * DK ** (-0.5)
            mixed_key, rows_key, scale_key = head_rows(
                columns(raw_ref, at_key, DK), taps_ref[:, at_key : at_key + DK], same, True
            )
            key = rows_key * scale_key
            mixed_value, value, _ = head_rows(
                columns(raw_ref, at_value, DV), taps_ref[:, at_value : at_value + DV], same, False
            )
            beta = sigmoid(pick(small, head))
            inverse, scores = inverse_ref[0, head], scores_ref[0, head]
            solved_keys, solved_values = keys_ref[0, head], values_ref[0, head]
            update, state = update_ref[0, head], state_ref[0, head]

            unit_at = (turn - micro) * heads + head
            grad_mixed, pull = kept_mixed[unit_at], line[1][unit_at]
            grad_update = kept_update[unit_at] + mm(key * to_end, pull)
            grad_solved_keys = -mm(grad_update, state, 1, 1)
            read = mm(grad_mixed, state, 1, 1)
            grad_query = gamma_in * read
            grad_gamma_in = row_sum(query * read)
            grad_scores = mm(grad_mixed, update, 1, 1)
            grad_inner = grad_scores * decay
            grad_query = grad_query + mm(grad_inner, key)
            grad_key = mm(grad_inner, query, 0, 0)
            written = mm(update, pull, 1, 1)
            grad_key = grad_key + to_end * written
            grad_to_end = row_sum(key * written) * to_end
            grad_all = jnp.sum(row_sum(pull * state), axis=0, keepdims=True) * gamma_all

            right_values = mm(inverse, grad_update, 0, 0)
            right_keys = mm(inverse, grad_solved_keys, 0, 0)
            grad_value = beta * right_values
            grad_beta = row_sum(value * right_values)
            along = row_sum(key * right_keys)
            grad_key = grad_key + (beta * gamma_in) * right_keys
            grad_beta = grad_beta + gamma_in * along
            grad_gamma_in = grad_gamma_in + beta * along
            inner = mm(key, key, 1, 1)
            grad_system = -(mm(right_values, solved_values, 1, 1) + mm(right_keys, solved_keys, 1, 1))
            grad_system = jnp.where(r > c, grad_system * decay, 0.0)
            grad_beta = grad_beta + row_sum(grad_system * inner)
            grad_system = beta * grad_system
            grad_log = grad_system * inner + grad_scores * scores
            grad_key = grad_key + mm(grad_system, key) + mm(grad_system, key, 0, 0)

            grad_cum = row_sum(grad_log - jnp.transpose(grad_log))
            grad_cum = grad_cum + grad_gamma_in * gamma_in - grad_to_end
            at_end = jnp.sum(grad_to_end, axis=0, keepdims=True) + grad_all
            cum_grad = jnp.where(lanes == heads + head, grad_cum, cum_grad)
            end_grad = jnp.where(lanes[0:1] == heads + head, at_end, end_grad)
            small_grad = jnp.where(lanes == head, grad_beta * beta * (1.0 - beta), small_grad)

            grad_rows = unit_backward(rows_query, scale_query, DK ** (-0.5), grad_query)
            finish(at_query, DK, silu_backward(mixed_query, grad_rows))
            grad_rows = unit_backward(rows_key, scale_key, 1.0, grad_key)
            finish(at_key, DK, silu_backward(mixed_key, grad_rows))
            finish(at_value, DV, silu_backward(mixed_value, grad_value))

        rate_grad = mm((r <= c).astype(F32), cum_grad, exact=True) + end_grad
        decay_grad = rate_grad * slopes
        empty = jnp.zeros((HALO, 128), F32)
        grad_raw_ref[0, :, at_small : at_small + 128] = jnp.concatenate(
            [empty, small_grad + decay_grad], axis=0
        ).astype(BF16)
        grad_small_ref[0:1] += jnp.sum(rate_grad * rates, axis=0, keepdims=True)
        grad_small_ref[1:2] += jnp.sum(decay_grad, axis=0, keepdims=True)
        part_ref[0] = lax.dot_general(
            grad_raw_ref[0], in_ref[...], (((1,), (1,)), ((), ())), preferred_element_type=F32
        ).astype(BF16)

    reached = turn - (depth - 1 - place.z)

    @pl.when(between(reached, 0, micro - 1))
    def _():
        for head in range(heads):
            unit = reached * heads + head
            receive, send = state_line(place, False, line, unit)
            pull = receive()
            send(lambda: mm(move_ref[unit], pull, 0, 0) + kept_local[unit])

    if count:
        for step, i in zip(steps[1:-1], scatter_turns(micro, len(steps) - 2)):
            at_turn(i, step)

    @pl.when(turn == 2 * micro - 1)
    def _():
        state_sent(place, False, line, micro * heads)
        for step in steps[-1:]:
            step()


def held_once(shape):
    zeros = (0,) * len(shape)
    return pl.BlockSpec(tuple(shape), lambda t: zeros, pipeline_mode=pl.Buffered(1))


def early(shape, micro, buffers=2):
    zeros = (0,) * (len(shape) - 1)
    return pl.BlockSpec(
        (1,) + tuple(shape[1:]),
        lambda t: (jnp.minimum(t, micro - 1),) + zeros,
        pipeline_mode=pl.Buffered(buffers),
    )


def later(shape, micro):
    zeros = (0,) * (len(shape) - 1)
    return pl.BlockSpec(
        (1,) + tuple(shape[1:]), lambda t: (jnp.maximum(t - micro, 0),) + zeros
    )


def delta_forward(block, seg_col, seg_row, in_gain, full_in, shared, heads, shards, collective):
    m, rows, _ = block.shape
    n = rows - HALO
    taps, gain, rate_log, rate_bias = shared
    depth = lax.axis_size("ctx")
    count = len(shards)
    units = m * heads
    prepared = [
        ((m, heads, n, n), F32),
        ((m, heads, n, n), F32),
        ((m, heads, n, DK), F32),
        ((m, heads, n, DV), F32),
        ((m, heads, n, DK), F32),
        ((m, heads, DK, DK), F32),
    ]
    mixed = [
        ((m, heads, DK, DV), F32),
        ((m, heads, n, DV), F32),
        ((m, heads, n, DV), F32),
        ((m, n, heads * DV), BF16),
    ]
    hidden = [(block.shape, BF16), ((m, rows, full_in.shape[1]), F32)]
    full = [((4 * depth,) + w.shape, w.dtype) for w in shards]
    held = [(n, n), (n, DK), (n, DV), (n, DK), (DK, DK), (DK, DV)]
    results = pl.pallas_call(
        functools.partial(forward_kernel, heads, depth, m, count),
        grid=(2 * m,),
        in_specs=[early(a.shape, m) for a in (block, seg_col, seg_row)]
        + [held_once(in_gain.shape), held_once(full_in.shape)]
        + [fixed(taps.shape), fixed(gain.shape), SCALARS, SCALARS]
        + [ANYWHERE] * count,
        out_specs=[early(shape, m) for shape, _ in prepared]
        + [later(shape, m) for shape, _ in mixed]
        + [early(shape, m) for shape, _ in hidden]
        + [ANYWHERE] * count,
        out_shape=shapes_of(prepared + mixed + hidden + full),
        scratch_shapes=[pltpu.VMEM((m, n, heads * DV), F32)]
        + [pltpu.VMEM((units,) + shape, F32) for shape in held]
        + state_scratch(units)
        + (gather_scratch([w.shape[1] for w in shards], depth) if count else []),
        compiler_params=pltpu.CompilerParams(
            collective_id=collective, has_side_effects=True, vmem_limit_bytes=48 * 2**20
        ),
    )(block, seg_col, seg_row, in_gain, full_in, taps, gain, rate_log, rate_bias, *shards)
    return results[:12], results[12:]


def delta_backward(seg_col, seg_row, full_in, shared, kept, grad, heads, grads, collective):
    inverse, scores, keys, values, enter, moves, state, update, mixed, _, hidden, raw = kept
    taps, gain, rate_log, rate_bias = shared
    m, n = grad.shape[:2]
    rows, cols = hidden.shape[1], full_in.shape[1]
    depth = lax.axis_size("ctx")
    count = len(grads)
    units = m * heads
    outs = [(hidden.shape, BF16), ((m, rows, cols), BF16)]
    outs = outs + [(taps.shape, F32), ((8, 128), F32), (gain.shape, F32)]
    specs = [later(hidden.shape, m), later((m, rows, cols), m)]
    specs = specs + [fixed(taps.shape), fixed((8, 128)), fixed(gain.shape)]
    scratch = [
        pltpu.VMEM((m, n, heads * DV), BF16),
        pltpu.VMEM((units, n, DV), F32),
        pltpu.VMEM((units, n, DV), F32),
        pltpu.VMEM((units, DK, DV), F32),
    ] + state_scratch(units)
    if count:
        widths = [a.shape[2] for a in grads]
        shard = grads[0].shape[1]
        outs = outs + [((shard, sum(widths)), F32)]
        specs = specs + [fixed((shard, sum(widths)))]
        scratch = scratch + scatter_scratch(widths, shard, depth)
    first = (scores, keys, enter)
    moves = moves.reshape(units, DK, DK)
    rest = (seg_col, seg_row, inverse, scores, keys, values, update, state)
    return pl.pallas_call(
        functools.partial(backward_kernel, heads, depth, m, count),
        grid=(2 * m,),
        in_specs=[early(grad.shape, m), early(mixed.shape, m)]
        + [pl.BlockSpec((1, rows, heads * DV), lambda t: (jnp.minimum(t, m - 1), 0, 2))]
        + [early(a.shape, m) for a in first]
        + [held_once(moves.shape)]
        + [later(a.shape, m) for a in rest + (raw,)]
        + [held_once(full_in.shape)]
        + [fixed(taps.shape), fixed(gain.shape), SCALARS, SCALARS]
        + [ANYWHERE] * count,
        out_specs=specs,
        out_shape=shapes_of(outs),
        scratch_shapes=scratch,
        compiler_params=pltpu.CompilerParams(
            collective_id=collective, has_side_effects=True, vmem_limit_bytes=62 * 2**20
        ),
    )(grad, mixed, raw, *first, moves, *rest, raw, full_in, taps, gain, rate_log, rate_bias, *grads)


def exchange(place, mine, theirs, sent, got, m):
    return remote(mine.at[m], theirs.at[m], sent.at[m], got.at[m], tp=1 - place.rank)


def middle_kernel(depth, micro, *refs):
    normed_ref, out_ref, block_ref, gain_ref, resid_ref, hidden_ref, mine, theirs, sent, got = refs
    place = Place(depth)
    turn = pl.program_id(0)

    @pl.when(turn == 0)
    def _():
        signal(tp=1 - place.rank)
        greeted(1)

    @pl.when(turn < micro)
    def _():
        mine[turn] = lax.dot_general(
            normed_ref[0], out_ref[...], (((1,), (1,)), ((), ())), preferred_element_type=F32
        )
        exchange(place, mine, theirs, sent, got, turn).start()

    @pl.when(turn >= 1)
    def _():
        m = turn - 1
        exchange(place, mine, theirs, sent, got, m).wait()
        resid = block_ref[0, HALO:].astype(F32) + (mine[m] + theirs[m])
        scale = inverse_root(jnp.mean(resid * resid, axis=1, keepdims=True) + 1e-06)
        resid_ref[0] = resid
        hidden_ref[0] = (resid * scale * gain_ref[...]).astype(BF16)


def back_kernel(depth, micro, count, *refs):
    pair_ref, full_ref, resid_ref, rows_ref, gain_ref, out_ref = refs[:6]
    g_refs, refs = refs[6 : 6 + count], refs[6 + count :]
    grad_resid_ref, grad_mix_ref, grad_normed_ref, grad_gain_ref = refs[:4]
    sum_refs, refs = refs[4 : 4 + (count > 0)], refs[4 + (count > 0) :]
    mine, theirs, sent, got = refs[:4]
    place = Place(depth)
    turn = pl.program_id(0)
    steps = []
    if count:
        load_all, steps = scatter_steps(place, g_refs, sum_refs[0], refs[4:])

    @pl.when(turn == 0)
    def _():
        if count:
            load_all()
            greeted(greet(place, True, tensor=True))
        else:
            signal(tp=1 - place.rank)
            greeted(1)
        for step in steps[:1]:
            step()
        grad_gain_ref[...] = jnp.zeros_like(grad_gain_ref)

    @pl.when(turn < micro)
    def _():
        mine[turn] = lax.dot_general(
            pair_ref[0], full_ref[...], (((1,), (1,)), ((), ())), preferred_element_type=F32
        )
        exchange(place, mine, theirs, sent, got, turn).start()

    @pl.when(turn >= 1)
    def _():
        m = turn - 1
        exchange(place, mine, theirs, sent, got, m).wait()
        grad = mine[m] + theirs[m]
        values = resid_ref[0]
        scale = inverse_root(jnp.mean(values * values, axis=1, keepdims=True) + 1e-06)
        unit = values * scale
        grad_gain_ref[...] += jnp.sum(grad * unit, axis=0, keepdims=True)
        grad = grad * gain_ref[...]
        moved = scale * (grad - unit * jnp.mean(grad * unit, axis=1, keepdims=True))
        grad_resid = rows_ref[0].astype(F32) + moved
        grad_mix = grad_resid.astype(BF16)
        grad_resid_ref[0] = grad_resid
        grad_mix_ref[0] = grad_mix
        grad_normed_ref[0] = jnp.dot(grad_mix, out_ref[...], preferred_element_type=F32)

    for i, step in enumerate(steps[1:-2]):
        at_turn(min(i, micro), step)

    @pl.when(turn == micro)
    def _():
        for step in steps[-2:]:
            step()


def behind(shape, micro):
    zeros = (0,) * (len(shape) - 1)
    return pl.BlockSpec((1,) + tuple(shape[1:]), lambda t: (jnp.maximum(t - 1, 0),) + zeros)


def middle(normed, full_out, block, gain, collective):
    m, n, _ = normed.shape
    features = full_out.shape[0]
    depth = lax.axis_size("ctx")
    outs = [((m, n, features), F32), ((m, n, features), BF16)]
    return pl.pallas_call(
        functools.partial(middle_kernel, depth, m),
        grid=(m + 1,),
        in_specs=[early(normed.shape, m), held_once(full_out.shape), behind(block.shape, m)]
        + [held_once(gain.shape)],
        out_specs=[behind(shape, m) for shape, _ in outs],
        out_shape=shapes_of(outs),
        scratch_shapes=[pltpu.VMEM((m, n, features), F32)] * 2 + [DMA((m,))] * 2,
        compiler_params=pltpu.CompilerParams(
            collective_id=collective, has_side_effects=True, vmem_limit_bytes=40 * 2**20
        ),
    )(normed, full_out, block, gain)


def back(pair, full_pair, resid, rows, gain, full_out, grads, collective):
    m, n, _ = pair.shape
    features, values = full_out.shape
    depth = lax.axis_size("ctx")
    count = len(grads)
    outs = [((m, n, features), F32), ((m, n, features), BF16), ((m, n, values), F32)]
    specs = [behind(shape, m) for shape, _ in outs] + [fixed(gain.shape)]
    outs = outs + [(gain.shape, F32)]
    scratch = [pltpu.VMEM((m, n, features), F32)] * 2 + [DMA((m,))] * 2
    if count:
        widths = [a.shape[2] for a in grads]
        shard = grads[0].shape[1]
        outs = outs + [((shard, sum(widths)), F32)]
        specs = specs + [fixed((shard, sum(widths)))]
        scratch = scratch + scatter_scratch(widths, shard, depth)
    return pl.pallas_call(
        functools.partial(back_kernel, depth, m, count),
        grid=(m + 1,),
        in_specs=[early(pair.shape, m), held_once(full_pair.shape)]
        + [behind(resid.shape, m), behind(rows.shape, m)]
        + [held_once(gain.shape), held_once(full_out.shape)]
        + [ANYWHERE] * count,
        out_specs=specs,
        out_shape=shapes_of(outs),
        scratch_shapes=scratch,
        compiler_params=pltpu.CompilerParams(
            collective_id=collective, has_side_effects=True, vmem_limit_bytes=56 * 2**20
        ),
    )(pair, full_pair, resid, rows, gain, full_out, *grads)


def dot(a, b, ca=1, cb=0, kind=F32):
    return lax.dot_general(a, b, (((ca,), (cb,)), ((), ())), preferred_element_type=F32).astype(
        kind
    )


def whole(shards):
    return [lax.all_gather(w, ("dp", "ctx")) for w in shards]


def summed(grads):
    both = jnp.concatenate([a.astype(F32) for a in grads], axis=2)
    return lax.psum_scatter(both, ("dp", "ctx"), scatter_dimension=0)


def on_device(
    tokens,
    segments,
    first_gain,
    query_weight,
    key_weight,
    value_weight,
    gate_weight,
    beta_weight,
    decay_weight,
    conv_query,
    conv_key,
    conv_value,
    decay_log,
    decay_bias,
    output_gain,
    out_weight,
    second_gain,
    ffn_gate,
    ffn_up,
    ffn_down,
    out_grad,
):
    rank = lax.axis_index("tp")
    place = lax.axis_index("ctx")
    depth = lax.axis_size("ctx")
    micro, _, n, width = tokens.shape
    heads = beta_weight.shape[1]
    keys, values, hidden = heads * DK, heads * DV, ffn_gate.shape[1]
    rows = HALO + n
    shard = query_weight.shape[0]
    blocks = lax.axis_size("dp") * depth
    plane = lax.axis_size("dp") == 4 and shard % 32 == 0

    padding = jnp.zeros((shard, 128 - 2 * heads), BF16)
    in_shards = [
        query_weight,
        key_weight,
        value_weight,
        gate_weight,
        jnp.concatenate([beta_weight, decay_weight, padding], axis=1),
    ]
    shards = [
        jnp.transpose(out_weight),
        jnp.concatenate([ffn_gate, ffn_up], axis=1),
        jnp.transpose(ffn_down),
    ]
    results = entry(tokens[:, 0], in_shards if plane else [], 0)
    token_block = results[0]
    (full_in,) = results[1:] if plane else whole([jnp.concatenate(in_shards, axis=1)])
    full_in = full_in.reshape(D, -1)

    seg_all = jnp.concatenate([jnp.full((micro, HALO), -1, jnp.int32), segments[:, 0]], axis=1)
    seg_here = lax.dynamic_slice_in_dim(seg_all, place * n, rows, 1).astype(F32)
    seg_col = jnp.broadcast_to(seg_here[:, :, None], (micro, rows, 128))
    seg_row = jnp.broadcast_to(seg_here[:, None, HALO:], (micro, 8, n))
    taps = jnp.concatenate(
        [
            lax.dynamic_slice_in_dim(a, rank * size, size, 1)
            for a, size in ((conv_query, keys), (conv_key, keys), (conv_value, values))
        ],
        axis=1,
    )
    rate_log = lax.dynamic_slice_in_dim(decay_log, rank * heads, heads, 0)
    rate_bias = lax.dynamic_slice_in_dim(decay_bias, rank * heads, heads, 0)
    gain = output_gain[None]
    shared = (taps, gain, rate_log, rate_bias)

    kept, full = delta_forward(
        token_block,
        seg_col,
        seg_row,
        first_gain[None],
        full_in,
        shared,
        heads,
        shards if plane else [],
        1,
    )
    normed = kept[9]
    full_out, full_pair, full_down = (
        a.reshape(D, -1) for a in (full if plane else whole(shards))
    )

    resid, hidden_mid = middle(normed, full_out, token_block, second_gain[None], 2)
    flat_mid = hidden_mid.reshape(micro * n, D)
    pair_pre = dot(flat_mid, full_pair)
    gate_pre, up_pre = pair_pre[:, :hidden], pair_pre[:, hidden:]
    slope = jax.nn.sigmoid(gate_pre)
    gate_act = gate_pre * slope
    activated = (gate_act * up_pre).astype(BF16)
    ffn_part = dot(activated, full_down, 1, 1, BF16)
    ffn_mine = lax.dynamic_slice_in_dim(ffn_part, rank * width, width, 1)
    ffn_theirs = swap(lax.dynamic_slice_in_dim(ffn_part, (1 - rank) * width, width, 1), 3)
    resid_mine = lax.dynamic_slice_in_dim(resid.reshape(micro * n, D), rank * width, width, 1)
    layer_out = (resid_mine + (ffn_mine.astype(F32) + ffn_theirs.astype(F32))).astype(BF16)

    grad_rows = out_grad[:, 0].reshape(micro * n, D)
    grad_act = dot(grad_rows, full_down)
    grad_gate = (grad_act * up_pre * slope * (1.0 + gate_pre * (1.0 - slope))).astype(BF16)
    grad_up = (grad_act * gate_act).astype(BF16)
    grad_pair = jnp.concatenate([grad_gate, grad_up], axis=1)

    def row_blocks(a):
        return a.reshape(blocks, shard, -1)

    results = back(
        grad_pair.reshape(micro, n, -1),
        full_pair,
        resid,
        out_grad[:, 0],
        second_gain[None],
        full_out,
        [],
        4,
    )
    grad_resid, grad_mix, grad_normed, grad_second = results[:4]
    late = [
        row_blocks(dot(grad_mix.reshape(micro * n, D), normed.reshape(micro * n, values), 0, 0, BF16)),
        row_blocks(dot(flat_mid, grad_pair, 0, 0, BF16)),
        row_blocks(dot(grad_rows, activated, 0, 0, BF16)),
    ]
    results = delta_backward(
        seg_col, seg_row, full_in, shared, kept, grad_normed, heads, late if plane else [], 5
    )
    in_part, grad_raw, grad_taps, grad_small, grad_gain = results[:5]
    sums = results[5] if plane else summed(late)
    flat_hidden = kept[10].reshape(micro * rows, D)
    in_grads = [row_blocks(dot(flat_hidden, grad_raw.reshape(micro * rows, -1), 0, 0, BF16))]

    results = leave(
        in_part,
        token_block,
        grad_resid,
        first_gain[None],
        (grad_second, grad_taps, grad_small, grad_gain),
        in_grads if plane else [],
        6,
    )
    token_grad, small = results[:2]
    decay_sums = small[11:13, : 128 * (H // heads)].reshape(2, -1, 128)[:, :, heads : 2 * heads]
    decay_sums = decay_sums.reshape(2, H)
    in_sums = results[2] if plane else summed(in_grads)

    edges = [0, keys, 2 * keys, 2 * keys + values, 2 * keys + 2 * values]
    edges = edges + [edges[-1] + heads, edges[-1] + 2 * heads]
    grad_in_weights = [in_sums[:, a:b] for a, b in zip(edges[:-1], edges[1:])]
    at = values
    return (
        layer_out.reshape(micro, 1, n, width),
        token_grad[:, None],
        small[0],
        *grad_in_weights,
        small[2:6, : H * DK],
        small[2:6, H * DK :],
        small[6:10],
        decay_sums[0],
        decay_sums[1],
        small[10, :DV],
        jnp.transpose(sums[:, :at]),
        small[1],
        sums[:, at : at + hidden],
        sums[:, at + hidden : at + 2 * hidden],
        jnp.transpose(sums[:, at + 2 * hidden :]),
    )


def solution(mesh):
    large = P(("dp", "ctx"), "tp")
    turned = P("tp", ("dp", "ctx"))
    spread = P(None, "dp", "ctx", "tp")
    in_specs = (
        (spread, P(None, "dp", None), P())
        + (large,) * 6
        + (P(),) * 6
        + (turned, P(), large, large, turned, P(None, "dp", "ctx", None))
    )
    out_specs = (
        (spread, spread, P())
        + (large,) * 6
        + (P(),) * 6
        + (turned, P(), large, large, turned)
    )
    return jax.shard_map(
        on_device, mesh=mesh, in_specs=in_specs, out_specs=out_specs, check_vma=False
    )
```
